1024 devices in a mesh: dp: 32 (over z), ctx: 16 (over x_hi, y, core), tp: 2 (over x_lo).
Axes of the slice: x: 4 (x_hi: 2, x_lo: 2; x = x_hi * 2 + x_lo), y: 4, z: 32, core: 2. Of those that a mesh axis runs over, the one named last changes fastest.
Arguments:
- queries: bfloat16 [32, 2048, 4096], P('dp', 'ctx', 'tp'), may hold values from -8 to 8
- keys_text: bfloat16 [32, 2048, 512], P('dp', 'ctx', 'tp'), may hold values from -8 to 8
- values_text: bfloat16 [32, 2048, 512], P('dp', 'ctx', 'tp'), may hold values from -6 to 6
- patch_rows: bfloat16 [32, 16, 64, 2, 512], P('dp', 'ctx', None, None, 'tp'), may hold values from -6 to 6
- patch_owner: int32 [32, 16, 64, 1], P('dp', 'ctx'), may hold values from 0 to 31; in each aligned block of 64 rows (0 to 63, 64 to 127, ..., all dimensions but the last counted through in order) at most 4 rows name the same one
- patch_place: int32 [32, 16, 64], P('dp', 'ctx'), may hold values from 0 to 127
- value_head: bfloat16 [4096], P('tp'), may hold values from -0.75 to 0.75
Outputs:
- attention: bfloat16 [32, 2048, 4096], P('dp', 'ctx', 'tp')
- value_out: float32 [32, 2048], P('dp', 'ctx')
The draws below stay inside these ranges and needn't reach their ends.
Inputs may be any that keep to these rules, and one draw needn't show every extreme that they name: `patch_owner`: among the rows of one vision shard at most 4 name the same sequence, and exactly 4 do in some shards. `patch_place`: rows that share an owner, a ctx index and a position are all added there.
All inputs are finite; a program needn't handle non-finite values.
Results may differ from the reference program's by a relative error of at most 0.0079.
Values may be sent and summed in bfloat16 or wider, within the bound.
No kernel may reach another device: no remote copies, remote signals or barrier semaphores. Data moves between devices by JAX's collectives and lax.ppermute only.
A program may use at most 32 MiB of HBM per device.

```python
import math
import jax
import jax.numpy as jnp
import numpy as np
from jax import lax

QHEADS = 32
KVHEADS = 4
HD = 128
TOK_DEV = 128
CAP = 4
LEN = 2048
PATCH_DEV = 64
N_DP = 32
N_CTX = 16


def draw_queries(key, part):
    own_key = jax.random.fold_in(key, 11)
    drawn = jnp.clip(jax.random.normal(own_key, (N_DP, LEN, QHEADS * HD), jnp.float32), -8.0, 8.0)
    return drawn.astype(jnp.bfloat16)


def draw_keys_text(key, part):
    own_key = jax.random.fold_in(key, 13)
    drawn = jnp.clip(jax.random.normal(own_key, (N_DP, LEN, KVHEADS * HD), jnp.float32), -8.0, 8.0)
    return drawn.astype(jnp.bfloat16)


def plant(array, key, low, high):
    longest = array.shape.index(max(array.shape))
    spots = []
    for shift in (0, 1):
        where = [jax.random.randint(jax.random.fold_in(key, axis), (), 0, length) for axis, length in enumerate(array.shape)]
        where[longest] = (where[longest] + shift) % array.shape[longest]
        spots.append(tuple(where))
    return array.at[spots[0]].set(low).at[spots[1]].set(high)


def block_levels(rng, dims, pieces, smallest, top_value):
    def one(dim, parts):
        draws = jax.random.uniform(jax.random.fold_in(jax.random.fold_in(rng, 6), dim), (parts,), jnp.float32, smallest / len(pieces), top_value / len(pieces))
        return jnp.repeat(jnp.exp(draws), dims[dim] // parts).reshape((-1,) + (1,) * (len(dims) - dim - 1))

    gain = one(*pieces[0])
    for cut in pieces[1:]:
        gain = gain * one(*cut)
    return gain


def routed_block(key, own, number, rows, count, top, most, lean):
    order = jax.random.permutation(key, count)
    packed, ordinary = shares(count, rows * top, most, lean, True), shares(count, rows * top, most, lean, False)
    places = jnp.arange(count)

    def named(lengths, turn):
        used = int((lengths > 0).sum())
        fixed = max(1, used // 4)
        shifted = fixed + (places - fixed + turn * (used - fixed)) % max(1, count - fixed)
        return jnp.zeros((count,), jnp.int32).at[order[jnp.where(places < fixed, places, shifted)]].set(jnp.asarray(lengths, jnp.int32))

    lengths = jnp.where(number % 4 == 0, named(packed, number // 4), named(ordinary, number - number // 4 - 1))
    mixed = jax.random.permutation(jax.random.fold_in(own, 3), count)
    source_of, receiver = mixed[0:count // 2 * 2:2], mixed[1:count // 2 * 2:2]
    slack = jnp.minimum(lengths[source_of] - 1, most - lengths[receiver]) // 2
    slack = jnp.where((source_of == order[0]) | (receiver == order[0]) | (lengths[receiver] == 0), 0, jnp.maximum(slack, 0))
    shifted = jax.random.randint(jax.random.fold_in(own, 4), (count // 2,), 0, 1 << 20) % (slack + 1)
    lengths = lengths.at[source_of].add(-shifted).at[receiver].add(shifted)
    items = jnp.searchsorted(jnp.cumsum(lengths), jnp.arange(rows * top), side="right").astype(jnp.int32)
    listing = items.reshape(top, rows).T
    listing = listing[jax.random.permutation(jax.random.fold_in(own, 1), rows)]
    turn = jax.random.randint(jax.random.fold_in(own, 2), (rows, 1), 0, top)
    return jnp.take_along_axis(listing, (jnp.arange(top)[None, :] + turn) % top, axis=1)


def shares(amount, total, bound, lean, full):
    portions = [(1 << 20) // math.isqrt(grade ** lean) + 1 for grade in range(1, amount + 1)]
    largest = bound if full else min(bound, max(-(-total // amount), total * portions[0] // sum(portions)))
    least = 1 if total - largest >= amount - 1 else 0
    holding, surplus = [largest] + [least] * (amount - 1), total - largest - least * (amount - 1)
    while surplus > 0:
        movable = [i for i in range(1, amount) if holding[i] < largest] or [i for i in range(1, amount) if holding[i] < bound]
        mass, left = sum([portions[i] for i in movable]), surplus
        for i in movable:
            more = min(bound - holding[i], max(1, left * portions[i] // mass), surplus)
            holding[i] = holding[i] + more
            surplus = surplus - more
    return np.array(holding)


def gaussian(stream_key, extent, scale, reach, cuts=(), kind=jnp.bfloat16):
    gain = block_levels(stream_key, extent, cuts, -0.22, 0.18) if cuts else 1.0
    values = jax.random.normal(stream_key, extent, jnp.float32) * scale * gain
    return jnp.minimum(jnp.maximum(values, -reach), reach).astype(kind)


def setup_inputs(seed: int = 0) -> dict:
    key_list = jax.random.split(jax.random.key(seed), 8)
    queries = draw_queries(jax.random.fold_in(key_list[7], 71), 0)
    keys_text = draw_keys_text(jax.random.fold_in(key_list[7], 71), 0)
    values_text = gaussian(key_list[2], (N_DP, LEN, KVHEADS * HD), 1.0, 6.0, ((0, 32), (1, 16), (2, 2)))
    patch_rows = gaussian(key_list[3], (N_DP, N_CTX, PATCH_DEV, 2, KVHEADS * HD), 1.0, 6.0, ((0, 32), (1, 16), (4, 2)))
    patch_owner_keys = jax.random.split(jax.random.fold_in(key_list[4], 1), N_DP * N_CTX * PATCH_DEV // PATCH_DEV)
    patch_owner_turns = jax.random.permutation(jax.random.fold_in(key_list[4], 3), N_DP * N_CTX * PATCH_DEV // PATCH_DEV)
    patch_owner = jax.vmap(lambda own, number: routed_block(jax.random.fold_in(key_list[4], 2), own, number, PATCH_DEV, N_DP, 1, CAP, 2))(patch_owner_keys, patch_owner_turns).reshape((N_DP, N_CTX, PATCH_DEV, 1))
    patch_place = plant(jax.random.randint(key_list[5], (N_DP, N_CTX, PATCH_DEV), 0, TOK_DEV), jax.random.fold_in(key_list[5], 1), 0, TOK_DEV - 1).astype(jnp.int32)
    value_head = gaussian(key_list[6], (QHEADS * HD,), 64 ** -0.5, 0.75, ((0, 2),))
    return dict(queries=queries, keys_text=keys_text, values_text=values_text, patch_rows=patch_rows, patch_owner=patch_owner, patch_place=patch_place, value_head=value_head)


def attend(queries_seq, keys_seq, values_seq):
    length = queries_seq.shape[0]
    groups = keys_seq.shape[1] // HD
    group_size = queries_seq.shape[1] // keys_seq.shape[1]
    score_scale = HD ** -0.5
    query_split = queries_seq.reshape(length, groups, group_size, HD).astype(jnp.float32)
    key_split = keys_seq.reshape(length, groups, HD).astype(jnp.float32)
    value_split = values_seq.reshape(length, groups, HD).astype(jnp.float32)
    block_rows = 512 if length % 512 == 0 else length
    results = []
    for lower in range(0, length, block_rows):
        upper = lower + block_rows
        scores = jnp.einsum("tgrd,sgd->tgrs", query_split[lower:upper], key_split[:upper]) * score_scale
        allowed = jnp.arange(upper, dtype=jnp.int32)[None, :] <= (lower + jnp.arange(block_rows, dtype=jnp.int32))[:, None]
        allowed = allowed[:, None, None, :]
        scores = jnp.where(allowed, scores, -1e30)
        row_max = jnp.max(scores, axis=-1)
        weights = jnp.where(allowed, jnp.exp(scores - row_max[..., None]), 0.0)
        denominator = jnp.sum(weights, axis=-1)
        rounded = weights.astype(jnp.bfloat16).astype(jnp.float32)
        numerator = jnp.einsum("tgrs,sgd->tgrd", rounded, value_split[:upper])
        mixed = numerator / denominator[..., None]
        results.append(mixed.reshape(block_rows, queries_seq.shape[1]).astype(jnp.bfloat16))
    return jnp.concatenate(results, axis=0)


def reference(queries, keys_text, values_text, patch_rows, patch_owner, patch_place, value_head):
    kv_width = keys_text.shape[2]
    owner_seq = patch_owner[..., 0]
    row_place = jnp.arange(N_CTX, dtype=jnp.int32)[None, :, None] * TOK_DEV + patch_place
    flat_index = (owner_seq * LEN + row_place).reshape(-1).astype(jnp.int32)
    key_add = patch_rows[:, :, :, 0, :].reshape(-1, kv_width).astype(jnp.float32)
    value_add = patch_rows[:, :, :, 1, :].reshape(-1, kv_width).astype(jnp.float32)
    merged_keys = keys_text.reshape(-1, kv_width).astype(jnp.float32).at[flat_index].add(key_add)
    merged_values = values_text.reshape(-1, kv_width).astype(jnp.float32).at[flat_index].add(value_add)
    merged_keys = merged_keys.astype(jnp.bfloat16).reshape(N_DP, LEN, kv_width)
    merged_values = merged_values.astype(jnp.bfloat16).reshape(N_DP, LEN, kv_width)

    def per_sequence(triple):
        return attend(triple[0], triple[1], triple[2])

    attention = lax.map(per_sequence, (queries, merged_keys, merged_values))
    value_out = jnp.dot(attention.reshape(-1, attention.shape[2]), value_head, preferred_element_type=jnp.float32)
    return attention, value_out.reshape(N_DP, LEN)
```

```python
import jax
import jax.numpy as jnp
from jax import lax
from jax.experimental import pallas as pl
from jax.experimental.pallas import tpu as pltpu
from jax.sharding import Mesh
from jax.sharding import PartitionSpec as P

HD = 128
CAP = 4
CHUNK = 512
LOG2E = 1.4426950408889634
NEVER = 512


def attend_kernel(first_ref, queries_ref, keys_values_ref, head_ref, out_ref, value_ref, top, mixed):
    rows, width = queries_ref.shape
    heads = width // HD
    factor = HD ** (-0.5) * LOG2E
    first = first_ref[0]
    top[...] = jnp.full(top.shape, -1e30, jnp.float32)
    mixed[...] = jnp.zeros(mixed.shape, jnp.float32)
    ones = jnp.ones((CHUNK, HD), jnp.bfloat16)

    def add_chunk(start, masked):
        keys = keys_values_ref[pl.ds(start, CHUNK), :HD]
        values = jnp.concatenate([keys_values_ref[pl.ds(start, CHUNK), HD:], ones], axis=1)
        if masked:
            allowed = start + lax.broadcasted_iota(jnp.int32, (rows, CHUNK), 1) <= (
                first + lax.broadcasted_iota(jnp.int32, (rows, CHUNK), 0)
            )
        for h in range(heads):
            scores = lax.dot_general(
                queries_ref[:, h * HD : (h + 1) * HD],
                keys,
                (((1,), (1,)), ((), ())),
                preferred_element_type=jnp.float32,
            )
            if masked:
                scores = jnp.where(allowed, scores, -1e30)
            before = top[:, h * HD : (h + 1) * HD]
            now = jnp.maximum(before, jnp.max(scores, axis=1, keepdims=True))
            weights = jnp.exp2((scores - now[:, :1]) * factor)
            shrink = jnp.exp2((before - now) * factor)
            top[:, h * HD : (h + 1) * HD] = now
            mixed[h] = mixed[h] * jnp.concatenate([shrink, shrink], axis=1) + jnp.dot(
                weights.astype(jnp.bfloat16), values, preferred_element_type=jnp.float32
            )

    whole = first // CHUNK

    def step(i, carry):
        add_chunk(pl.multiple_of(i * CHUNK, CHUNK), False)
        return carry

    lax.fori_loop(0, whole, step, 0)
    add_chunk(pl.multiple_of(whole * CHUNK, CHUNK), True)
    value = jnp.zeros((rows, HD), jnp.float32)
    for h in range(heads):
        total = mixed[h]
        out = (total[:, :HD] / total[:, HD:]).astype(jnp.bfloat16)
        out_ref[:, h * HD : (h + 1) * HD] = out
        value = value + out.astype(jnp.float32) * head_ref[:, h * HD : (h + 1) * HD]
    value_ref[...] = lax.dot_general(
        jnp.ones((8, HD), jnp.float32),
        value,
        (((1,), (1,)), ((), ())),
        preferred_element_type=jnp.float32,
        precision=lax.Precision.HIGHEST,
    )


def attend(first, queries, keys_values, head):
    rows, width = queries.shape
    length = keys_values.shape[0]
    vmem = pl.BlockSpec(memory_space=pltpu.VMEM)
    return pl.pallas_call(
        attend_kernel,
        out_shape=(
            jax.ShapeDtypeStruct((rows, width), jnp.bfloat16),
            jax.ShapeDtypeStruct((8, rows), jnp.float32),
        ),
        in_specs=[pl.BlockSpec(memory_space=pltpu.SMEM), vmem, vmem, vmem],
        out_specs=(vmem, vmem),
        scratch_shapes=[
            pltpu.VMEM((rows, width), jnp.float32),
            pltpu.VMEM((width // HD, rows, 2 * HD), jnp.float32),
        ],
        compiler_params=pltpu.CompilerParams(vmem_limit_bytes=32 * 2**20),
        cost_estimate=pl.CostEstimate(
            flops=4 * rows * width * length, bytes_accessed=4 * rows * width, transcendentals=rows * width * length // HD
        ),
    )(first, queries, keys_values, head)


def body(queries, keys_text, values_text, patch_rows, patch_owner, patch_place, value_head):
    rows = queries.shape[1]
    half = queries.shape[2] // 2
    dp_count = lax.axis_size("dp")
    chip_count = lax.axis_size("xh") * lax.axis_size("y")
    core = lax.axis_index("co")
    chip = lax.axis_index("xh") * lax.axis_size("y") + lax.axis_index("y")
    swap = [(0, 1), (1, 0)]

    owner = patch_owner[0, 0, :, 0]
    place = patch_place[0, 0]
    count = owner.shape[0]
    earlier = jnp.arange(count)[:, None] < jnp.arange(count)[None, :]
    rank = jnp.sum(jnp.where(earlier & (owner[:, None] == owner[None, :]), 1, 0), axis=0)
    slots = dp_count * CAP
    select = jnp.arange(slots, dtype=jnp.int32)[:, None] == (owner * CAP + rank)[None, :]
    slot_place = jnp.sum(jnp.where(select, place[None, :] - NEVER, 0), axis=1) + NEVER
    packed = jnp.dot(
        select.astype(jnp.bfloat16),
        patch_rows[0, 0].reshape(count, 4 * HD),
        preferred_element_type=jnp.float32,
    ).astype(jnp.bfloat16)
    packed = packed.reshape(dp_count, CAP, 2, 2, HD).transpose(0, 3, 1, 2, 4)
    places = jnp.broadcast_to(
        slot_place.reshape(dp_count, 1, CAP, 1, 1).astype(jnp.bfloat16), (dp_count, 2, CAP, 1, HD)
    )
    packed = jnp.concatenate([packed, places], axis=3).reshape(dp_count * 2, CAP, 3 * HD)
    arrived = lax.all_to_all(packed, ("dp", "co"), 0, 0, tiled=True)
    arrived = arrived.reshape(dp_count * 2 * CAP, 3 * HD)

    text = jnp.concatenate([keys_text[0], values_text[0]], axis=1)
    text = text.reshape(rows, 2, 2, HD)
    other_text = lax.dynamic_index_in_dim(text, 1 - core, 2, False).reshape(rows, 2 * HD)
    own_text = lax.dynamic_index_in_dim(text, core, 2, False).reshape(rows, 2 * HD)
    both_queries = queries[0]
    other_queries = lax.dynamic_slice_in_dim(both_queries, (1 - core) * half, half, 1)
    own_queries = lax.dynamic_slice_in_dim(both_queries, core * half, half, 1)
    got_text = lax.ppermute(other_text, "co", swap)
    got_queries = lax.ppermute(other_queries, "co", swap)
    head = lax.dynamic_slice_in_dim(value_head, core * half, half, 0)[None].astype(jnp.float32)
    both_text = jnp.where(
        core == 0,
        jnp.concatenate([own_text, got_text], axis=0),
        jnp.concatenate([got_text, own_text], axis=0),
    )

    sender = (jnp.arange(dp_count * 2 * CAP, dtype=jnp.int32) // CAP) % 2
    token = arrived[:, 2 * HD].astype(jnp.int32) + sender * rows
    token = jnp.where(arrived[:, 2 * HD] < rows, token, NEVER)
    landing = (jnp.arange(2 * rows, dtype=jnp.int32)[:, None] == token[None, :]).astype(jnp.bfloat16)
    merged = (
        both_text.astype(jnp.float32)
        + jnp.dot(landing, arrived[:, : 2 * HD], preferred_element_type=jnp.float32)
    ).astype(jnp.bfloat16)
    keys_values = lax.all_to_all(
        jnp.broadcast_to(merged[None], (chip_count, *merged.shape)), ("xh", "y"), 0, 0, tiled=True
    ).reshape(chip_count * 2 * rows, 2 * HD)

    start = chip * (2 * rows)
    other_out, other_value = attend((start + (1 - core) * rows)[None], got_queries, keys_values, head)
    own_out, own_value = attend((start + core * rows)[None], own_queries, keys_values, head)
    got_out = lax.ppermute(other_out, "co", swap)
    got_value = lax.ppermute(other_value[0], "co", swap)
    attention = jnp.where(
        core == 0,
        jnp.concatenate([own_out, got_out], axis=1),
        jnp.concatenate([got_out, own_out], axis=1),
    )
    partial_value = own_value[0] + got_value
    value_out = partial_value + lax.ppermute(partial_value, "tp", swap)
    return attention[None], value_out[None]


def solution(mesh):
    dp, ctx, tp = mesh.devices.shape
    wide = Mesh(mesh.devices.reshape(dp, 2, ctx // 4, 2, tp), ("dp", "xh", "y", "co", "tp"))
    ctx = ("xh", "y", "co")
    in_specs = (
        P("dp", ctx, "tp"),
        P("dp", ctx, "tp"),
        P("dp", ctx, "tp"),
        P("dp", ctx, None, None, "tp"),
        P("dp", ctx, None, None),
        P("dp", ctx, None),
        P("tp"),
    )
    out_specs = (P("dp", ctx, "tp"), P("dp", ctx))
    return jax.shard_map(body, mesh=wide, in_specs=in_specs, out_specs=out_specs, check_vma=False)
```

```python
import jax
import jax.numpy as jnp
from jax import lax
from jax.experimental import pallas as pl
from jax.experimental.pallas import tpu as pltpu
from jax.sharding import Mesh
from jax.sharding import PartitionSpec as P

HD = 128
CAP = 4
CHUNK = 512
LOG2E = 1.4426950408889634


def column(row):
    count = row.shape[1]
    same = lax.broadcasted_iota(jnp.int32, (count, count), 0) == lax.broadcasted_iota(
        jnp.int32, (count, count), 1
    )
    return jnp.sum(jnp.where(same, row, 0), axis=1, keepdims=True)


def pack_kernel(patch_ref, owner_ref, place_ref, out_ref):
    owner, place = owner_ref[...], place_ref[...]
    count = owner.shape[1]
    owner_column = column(owner)
    earlier = lax.broadcasted_iota(jnp.int32, (count, count), 1) < lax.broadcasted_iota(
        jnp.int32, (count, count), 0
    )
    rank = jnp.sum(jnp.where(earlier & (owner_column == owner), 1, 0), axis=1, keepdims=True)
    target = owner_column * CAP + rank
    patch, row = (
        lax.broadcasted_iota(jnp.int32, (count, 2 * count), 0),
        lax.broadcasted_iota(jnp.int32, (count, 2 * count), 1),
    )
    target = jnp.sum(jnp.where(patch == row // 2, target, 0), axis=0, keepdims=True)
    row, patch = (
        lax.broadcasted_iota(jnp.int32, (2 * count, count), 0),
        lax.broadcasted_iota(jnp.int32, (2 * count, count), 1),
    )
    code = jnp.sum(jnp.where(patch == row // 2, place + 1, 0), axis=1, keepdims=True)
    rows = out_ref.shape[0]
    out, row = (
        lax.broadcasted_iota(jnp.int32, (rows, 2 * count), 0),
        lax.broadcasted_iota(jnp.int32, (rows, 2 * count), 1),
    )
    select = (out // 2 == target) & (out % 2 == row % 2)
    held = jnp.concatenate(
        [
            patch_ref[...],
            jnp.broadcast_to(code.astype(jnp.float32), (2 * count, HD)).astype(jnp.bfloat16),
        ],
        axis=1,
    )
    select = jnp.where(select, 1.0, 0.0).astype(jnp.bfloat16)
    out_ref[...] = jnp.dot(select, held, preferred_element_type=jnp.float32).astype(jnp.bfloat16)


def pack(patch_rows, owner, place, sequences):
    vmem = pl.BlockSpec(memory_space=pltpu.VMEM)
    return pl.pallas_call(
        pack_kernel,
        out_shape=jax.ShapeDtypeStruct((sequences * CAP * 2, patch_rows.shape[1] + HD), jnp.bfloat16),
        in_specs=[vmem, vmem, vmem],
        out_specs=vmem,
    )(patch_rows, owner, place)


def attend_kernel(first_ref, queries_ref, keys_values_ref, head_ref, out_ref, *value_ref):
    rows, width = queries_ref.shape
    length = keys_values_ref.shape[0]
    factor = HD ** (-0.5) * LOG2E
    first = first_ref[0]

    def attend_first(count):
        keys = keys_values_ref[:count, :HD]
        values = jnp.concatenate(
            [keys_values_ref[:count, HD:], jnp.ones((count, HD), jnp.bfloat16)], axis=1
        )
        whole = count - CHUNK
        allowed = whole + lax.broadcasted_iota(jnp.int32, (rows, CHUNK), 1) <= (
            first + lax.broadcasted_iota(jnp.int32, (rows, CHUNK), 0)
        )
        value = jnp.zeros((rows, HD), jnp.float32)
        for lower in range(0, width, HD):
            scores = lax.dot_general(
                queries_ref[:, lower : lower + HD],
                keys,
                (((1,), (1,)), ((), ())),
                preferred_element_type=jnp.float32,
            )
            last = jnp.where(allowed, scores[:, whole:], -1e30)
            scores = jnp.concatenate([scores[:, :whole], last], axis=1) if whole else last
            top = jnp.max(scores, axis=1, keepdims=True)
            weights = jnp.exp2((scores - top) * factor).astype(jnp.bfloat16)
            mixed = jnp.dot(weights, values, preferred_element_type=jnp.float32)
            out = (mixed[:, :HD] / mixed[:, HD:]).astype(jnp.bfloat16)
            out_ref[:rows, lower : lower + HD] = out
            value = value + out.astype(jnp.float32) * head_ref[:, lower : lower + HD]
        total = lax.dot_general(
            jnp.ones((16, HD), jnp.float32),
            value,
            (((1,), (1,)), ((), ())),
            preferred_element_type=jnp.float32,
            precision=lax.Precision.HIGHEST,
        )
        if value_ref:
            value_ref[0][...] = total
        else:
            row = lax.broadcasted_iota(jnp.int32, total.shape, 0)
            high = total.astype(jnp.bfloat16).astype(jnp.float32)
            middle = (total - high).astype(jnp.bfloat16).astype(jnp.float32)
            pieces = jnp.where(row == 0, high, jnp.where(row == 1, middle, total - high - middle))
            out_ref[rows:, :HD] = pieces.astype(jnp.bfloat16)
            out_ref[rows:, HD:] = jnp.zeros((16, width - HD), jnp.bfloat16)

    for i in range(length // CHUNK):

        @pl.when(first // CHUNK == i)
        def _():
            attend_first((i + 1) * CHUNK)


def attend(first, queries, keys_values, head, sums_apart):
    rows, width = queries.shape
    length = keys_values.shape[0]
    vmem = pl.BlockSpec(memory_space=pltpu.VMEM)
    out_shape = [jax.ShapeDtypeStruct((rows if sums_apart else rows + 16, width), jnp.bfloat16)]
    if sums_apart:
        out_shape.append(jax.ShapeDtypeStruct((16, rows), jnp.float32))
    return pl.pallas_call(
        attend_kernel,
        out_shape=out_shape,
        in_specs=[pl.BlockSpec(memory_space=pltpu.SMEM), vmem, vmem, vmem],
        out_specs=[vmem] * len(out_shape),
        compiler_params=pltpu.CompilerParams(vmem_limit_bytes=32 * 2**20),
        cost_estimate=pl.CostEstimate(
            flops=4 * rows * width * length, bytes_accessed=4 * rows * width, transcendentals=rows * width * length // HD
        ),
    )(first, queries, keys_values, head)


def body(queries, keys_text, values_text, patch_rows, patch_owner, patch_place, value_head):
    rows = queries.shape[1]
    half = queries.shape[2] // 2
    dp_count = lax.axis_size("dp")
    chip_count = lax.axis_size("xh") * lax.axis_size("y")
    core = lax.axis_index("co")
    chip = lax.axis_index("xh") * lax.axis_size("y") + lax.axis_index("y")
    swap = [(0, 1), (1, 0)]
    count = patch_rows.shape[2]

    packed = pack(
        patch_rows.reshape(count * 2, 2 * HD),
        patch_owner.reshape(1, count),
        patch_place.reshape(1, count),
        dp_count,
    )
    arrived = lax.all_to_all(packed.reshape(dp_count, CAP * 2, 3 * HD), "dp", 0, 0, tiled=True)
    arrived = arrived.reshape(dp_count * CAP * 2, 3 * HD)
    code = arrived[:, 2 * HD].astype(jnp.int32)
    is_value = jnp.arange(code.shape[0], dtype=jnp.int32) % 2
    lands = (jnp.arange(rows, dtype=jnp.int32)[:, None] + 1) == code[None, :]

    def merge(text, wanted):
        landing = jnp.where(lands & (is_value == wanted)[None, :], 1.0, 0.0).astype(jnp.bfloat16)
        added = jnp.dot(landing, arrived[:, : 2 * HD], preferred_element_type=jnp.float32)
        return (text[0].astype(jnp.float32) + added).astype(jnp.bfloat16)

    merged_keys, merged_values = merge(keys_text, 0), merge(values_text, 1)

    def of_head(which):
        return jnp.concatenate(
            [
                jnp.where(which == 0, tensor[:, :HD], tensor[:, HD:])
                for tensor in (merged_keys, merged_values)
            ],
            axis=1,
        )

    own_merged = of_head(core)
    got_merged = lax.ppermute(of_head(1 - core), "co", swap)
    merged = jnp.where(
        core == 0,
        jnp.concatenate([own_merged, got_merged], axis=0),
        jnp.concatenate([got_merged, own_merged], axis=0),
    )
    other_queries = lax.dynamic_slice_in_dim(queries[0], (1 - core) * half, half, 1)
    own_queries = lax.dynamic_slice_in_dim(queries[0], core * half, half, 1)
    got_queries = lax.ppermute(other_queries, "co", swap)
    head = lax.dynamic_slice_in_dim(value_head, core * half, half, 0)[None].astype(jnp.float32)

    keys_values = lax.all_to_all(
        jnp.broadcast_to(merged[None], (chip_count, *merged.shape)), ("xh", "y"), 0, 0, tiled=True
    ).reshape(chip_count * 2 * rows, 2 * HD)

    start = chip * (2 * rows)
    (other_out,) = attend((start + (1 - core) * rows)[None], got_queries, keys_values, head, False)
    own_out, own_value = attend((start + core * rows)[None], own_queries, keys_values, head, True)
    got_out = lax.ppermute(other_out, "co", swap)
    got_value = jnp.sum(got_out[rows : rows + 3, :HD].astype(jnp.float32), axis=0)
    attention = jnp.where(
        core == 0,
        jnp.concatenate([own_out, got_out[:rows]], axis=1),
        jnp.concatenate([got_out[:rows], own_out], axis=1),
    )
    partial_value = own_value[0] + got_value
    far_value = lax.ppermute(partial_value, "tp", swap)
    attention, far_value = lax.optimization_barrier((attention, far_value))
    return attention[None], (partial_value + far_value)[None]


def solution(mesh):
    dp, ctx, tp = mesh.devices.shape
    wide = Mesh(mesh.devices.reshape(dp, 2, ctx // 4, 2, tp), ("dp", "xh", "y", "co", "tp"))
    ctx = ("xh", "y", "co")
    in_specs = (
        P("dp", ctx, "tp"),
        P("dp", ctx, "tp"),
        P("dp", ctx, "tp"),
        P("dp", ctx, None, None, "tp"),
        P("dp", ctx, None, None),
        P("dp", ctx, None),
        P("tp"),
    )
    out_specs = (P("dp", ctx, "tp"), P("dp", ctx))
    return jax.shard_map(body, mesh=wide, in_specs=in_specs, out_specs=out_specs, check_vma=False)
```

```python
import jax
import jax.numpy as jnp
from jax import lax
from jax.experimental import pallas as pl
from jax.experimental.pallas import tpu as pltpu
from jax.sharding import Mesh
from jax.sharding import PartitionSpec as P

HD = 128
CAP = 4
CHUNK = 512
LOG2E = 1.4426950408889634


def column(row):
    count = row.shape[1]
    same = lax.broadcasted_iota(jnp.int32, (count, count), 0) == lax.broadcasted_iota(
        jnp.int32, (count, count), 1
    )
    return jnp.sum(jnp.where(same, row, 0), axis=1, keepdims=True)


def pack_kernel(patch_ref, owner_ref, place_ref, out_ref):
    owner, place = owner_ref[...], place_ref[...]
    count = owner.shape[1]
    owner_column = column(owner)
    earlier = lax.broadcasted_iota(jnp.int32, (count, count), 0) < lax.broadcasted_iota(
        jnp.int32, (count, count), 1
    )
    rank = jnp.sum(jnp.where(earlier & (owner_column == owner), 1, 0), axis=0, keepdims=True)
    target = owner * CAP + rank
    code = jnp.broadcast_to((column(place) + 1).astype(jnp.float32), (count, HD)).astype(jnp.bfloat16)
    row = lax.broadcasted_iota(jnp.int32, (out_ref.shape[0], count), 0)
    packed = jnp.zeros(out_ref.shape, jnp.float32)
    for which in range(2):
        select = jnp.where((row // 2 == target) & (row % 2 == which), 1.0, 0.0).astype(jnp.bfloat16)
        held = jnp.concatenate([patch_ref[:, which, :], code], axis=1)
        packed = packed + jnp.dot(select, held, preferred_element_type=jnp.float32)
    out_ref[...] = packed.astype(jnp.bfloat16)


def pack(patch_rows, owner, place, sequences):
    vmem = pl.BlockSpec(memory_space=pltpu.VMEM)
    return pl.pallas_call(
        pack_kernel,
        out_shape=jax.ShapeDtypeStruct((sequences * CAP * 2, patch_rows.shape[2] + HD), jnp.bfloat16),
        in_specs=[vmem, vmem, vmem],
        out_specs=vmem,
    )(patch_rows, owner, place)


def attend_kernel(first_ref, queries_ref, keys_values_ref, head_ref, out_ref, *value_ref):
    rows, width = queries_ref.shape
    length = keys_values_ref.shape[0]
    factor = HD ** (-0.5) * LOG2E
    first = first_ref[0]

    def attend_first(count):
        keys = keys_values_ref[:count, :HD]
        values = jnp.concatenate(
            [keys_values_ref[:count, HD:], jnp.ones((count, HD), jnp.bfloat16)], axis=1
        )
        whole = count - CHUNK
        allowed = whole + lax.broadcasted_iota(jnp.int32, (rows, CHUNK), 1) <= (
            first + lax.broadcasted_iota(jnp.int32, (rows, CHUNK), 0)
        )
        value = jnp.zeros((rows, HD), jnp.float32)
        for lower in range(0, width, HD):
            scores = lax.dot_general(
                queries_ref[:, lower : lower + HD],
                keys,
                (((1,), (1,)), ((), ())),
                preferred_element_type=jnp.float32,
            )
            last = jnp.where(allowed, scores[:, whole:], -1e30)
            scores = jnp.concatenate([scores[:, :whole], last], axis=1) if whole else last
            top = jnp.max(scores, axis=1, keepdims=True)
            weights = jnp.exp2((scores - top) * factor).astype(jnp.bfloat16)
            mixed = jnp.dot(weights, values, preferred_element_type=jnp.float32)
            out = (mixed[:, :HD] / mixed[:, HD:]).astype(jnp.bfloat16)
            out_ref[:rows, lower : lower + HD] = out
            value = value + out.astype(jnp.float32) * head_ref[:, lower : lower + HD]
        total = lax.dot_general(
            jnp.ones((16, HD), jnp.float32),
            value,
            (((1,), (1,)), ((), ())),
            preferred_element_type=jnp.float32,
            precision=lax.Precision.HIGHEST,
        )
        if value_ref:
            value_ref[0][...] = total
        else:
            row = lax.broadcasted_iota(jnp.int32, total.shape, 0)
            high = total.astype(jnp.bfloat16).astype(jnp.float32)
            middle = (total - high).astype(jnp.bfloat16).astype(jnp.float32)
            pieces = jnp.where(row == 0, high, jnp.where(row == 1, middle, total - high - middle))
            out_ref[rows:, :HD] = pieces.astype(jnp.bfloat16)
            out_ref[rows:, HD:] = jnp.zeros((16, width - HD), jnp.bfloat16)

    for i in range(length // CHUNK):

        @pl.when(first // CHUNK == i)
        def _():
            attend_first((i + 1) * CHUNK)


def attend(first, queries, keys_values, head, sums_apart):
    rows, width = queries.shape
    length = keys_values.shape[0]
    vmem = pl.BlockSpec(memory_space=pltpu.VMEM)
    out_shape = [jax.ShapeDtypeStruct((rows if sums_apart else rows + 16, width), jnp.bfloat16)]
    if sums_apart:
        out_shape.append(jax.ShapeDtypeStruct((16, rows), jnp.float32))
    return pl.pallas_call(
        attend_kernel,
        out_shape=out_shape,
        in_specs=[pl.BlockSpec(memory_space=pltpu.SMEM), vmem, vmem, vmem],
        out_specs=[vmem] * len(out_shape),
        compiler_params=pltpu.CompilerParams(vmem_limit_bytes=32 * 2**20),
        cost_estimate=pl.CostEstimate(
            flops=4 * rows * width * length, bytes_accessed=4 * rows * width, transcendentals=rows * width * length // HD
        ),
    )(first, queries, keys_values, head)


def body(queries, keys_text, values_text, patch_rows, patch_owner, patch_place, value_head):
    rows = queries.shape[1]
    half = queries.shape[2] // 2
    dp_count = lax.axis_size("dp")
    chip_count = lax.axis_size("xh") * lax.axis_size("y")
    core = lax.axis_index("co")
    chip = lax.axis_index("xh") * lax.axis_size("y") + lax.axis_index("y")
    swap = [(0, 1), (1, 0)]
    count = patch_rows.shape[2]

    packed = pack(
        patch_rows[0, 0],
        patch_owner.reshape(1, count),
        patch_place.reshape(1, count),
        dp_count,
    )
    arrived = lax.all_to_all(packed.reshape(dp_count, CAP * 2, 3 * HD), "dp", 0, 0, tiled=True)
    arrived = arrived.reshape(dp_count * CAP * 2, 3 * HD)
    other_queries = lax.dynamic_slice_in_dim(queries[0], (1 - core) * half, half, 1)
    own_queries = lax.dynamic_slice_in_dim(queries[0], core * half, half, 1)
    got_queries = lax.ppermute(other_queries, "co", swap)
    head = lax.dynamic_slice_in_dim(value_head, core * half, half, 0)[None].astype(jnp.float32)
    text = jnp.concatenate([keys_text[0], values_text[0]], axis=1)
    arrived, got_queries, own_queries, head, text = lax.optimization_barrier(
        (arrived, got_queries, own_queries, head, text)
    )

    code = arrived[:, 2 * HD].astype(jnp.int32)
    is_value = jnp.arange(code.shape[0], dtype=jnp.int32) % 2
    lands = (jnp.arange(rows, dtype=jnp.int32)[:, None] + 1) == code[None, :]

    def added(wanted):
        landing = jnp.where(lands & (is_value == wanted)[None, :], 1.0, 0.0).astype(jnp.bfloat16)
        return jnp.dot(landing, arrived[:, : 2 * HD], preferred_element_type=jnp.float32)

    merged_keys = (text[:, : 2 * HD].astype(jnp.float32) + added(0)).astype(jnp.bfloat16)
    merged_values = (text[:, 2 * HD :].astype(jnp.float32) + added(1)).astype(jnp.bfloat16)

    def of_head(which):
        return jnp.concatenate(
            [
                jnp.where(which == 0, tensor[:, :HD], tensor[:, HD:])
                for tensor in (merged_keys, merged_values)
            ],
            axis=1,
        )

    own_merged = of_head(core)
    got_merged = lax.ppermute(of_head(1 - core), "co", swap)
    merged = jnp.where(
        core == 0,
        jnp.concatenate([own_merged, got_merged], axis=0),
        jnp.concatenate([got_merged, own_merged], axis=0),
    )
    keys_values = lax.all_to_all(
        jnp.broadcast_to(merged[None], (chip_count, *merged.shape)), ("xh", "y"), 0, 0, tiled=True
    ).reshape(chip_count * 2 * rows, 2 * HD)

    start = chip * (2 * rows)
    (other_out,) = attend((start + (1 - core) * rows)[None], got_queries, keys_values, head, False)
    own_out, own_value = attend((start + core * rows)[None], own_queries, keys_values, head, True)
    got_out = lax.ppermute(other_out, "co", swap)
    got_value = jnp.sum(got_out[rows : rows + 3, :HD].astype(jnp.float32), axis=0)
    attention = jnp.where(
        core == 0,
        jnp.concatenate([own_out, got_out[:rows]], axis=1),
        jnp.concatenate([got_out[:rows], own_out], axis=1),
    )
    partial_value = own_value[0] + got_value
    far_value = lax.ppermute(partial_value, "tp", swap)
    attention, far_value = lax.optimization_barrier((attention, far_value))
    return attention[None], (partial_value + far_value)[None]


def solution(mesh):
    dp, ctx, tp = mesh.devices.shape
    wide = Mesh(mesh.devices.reshape(dp, 2, ctx // 4, 2, tp), ("dp", "xh", "y", "co", "tp"))
    ctx = ("xh", "y", "co")
    in_specs = (
        P("dp", ctx, "tp"),
        P("dp", ctx, "tp"),
        P("dp", ctx, "tp"),
        P("dp", ctx, None, None, "tp"),
        P("dp", ctx, None, None),
        P("dp", ctx, None),
        P("tp"),
    )
    out_specs = (P("dp", ctx, "tp"), P("dp", ctx))
    return jax.shard_map(body, mesh=wide, in_specs=in_specs, out_specs=out_specs, check_vma=False)
```

```python
import jax
import jax.numpy as jnp
from jax import lax
from jax.experimental import pallas as pl
from jax.experimental.pallas import tpu as pltpu
from jax.sharding import Mesh
from jax.sharding import PartitionSpec as P

HD = 128
CAP = 4
CHUNK = 512
LOG2E = 1.4426950408889634


def column(row):
    count = row.shape[1]
    same = lax.broadcasted_iota(jnp.int32, (count, count), 0) == lax.broadcasted_iota(
        jnp.int32, (count, count), 1
    )
    return jnp.sum(jnp.where(same, row, 0), axis=1, keepdims=True)


def pack_kernel(patch_ref, owner_ref, place_ref, out_ref):
    owner, place = owner_ref[...], place_ref[...]
    count = owner.shape[1]
    owner_column = column(owner)
    earlier = lax.broadcasted_iota(jnp.int32, (count, count), 0) < lax.broadcasted_iota(
        jnp.int32, (count, count), 1
    )
    rank = jnp.sum(jnp.where(earlier & (owner_column == owner), 1, 0), axis=0, keepdims=True)
    target = owner * CAP + rank
    code = jnp.broadcast_to((column(place) + 1).astype(jnp.float32), (count, HD)).astype(jnp.bfloat16)
    row = lax.broadcasted_iota(jnp.int32, (out_ref.shape[0], count), 0)
    packed = jnp.zeros(out_ref.shape, jnp.float32)
    for which in range(2):
        select = jnp.where((row // 2 == target) & (row % 2 == which), 1.0, 0.0).astype(jnp.bfloat16)
        held = jnp.concatenate([patch_ref[:, which, :], code], axis=1)
        packed = packed + jnp.dot(select, held, preferred_element_type=jnp.float32)
    out_ref[...] = packed.astype(jnp.bfloat16)


def pack(patch_rows, owner, place, sequences):
    vmem = pl.BlockSpec(memory_space=pltpu.VMEM)
    return pl.pallas_call(
        pack_kernel,
        out_shape=jax.ShapeDtypeStruct((sequences * CAP * 2, patch_rows.shape[2] + HD), jnp.bfloat16),
        in_specs=[vmem, vmem, vmem],
        out_specs=vmem,
    )(patch_rows, owner, place)


def attend_kernel(first_ref, queries_ref, keys_values_ref, head_ref, out_ref, *value_ref):
    rows, width = queries_ref.shape
    length = keys_values_ref.shape[0]
    factor = HD ** (-0.5) * LOG2E
    first = first_ref[0]

    def attend_first(count):
        keys = keys_values_ref[:count, :HD]
        values = jnp.concatenate(
            [keys_values_ref[:count, HD:], jnp.ones((count, HD), jnp.bfloat16)], axis=1
        )
        whole = count - CHUNK
        allowed = whole + lax.broadcasted_iota(jnp.int32, (rows, CHUNK), 1) <= (
            first + lax.broadcasted_iota(jnp.int32, (rows, CHUNK), 0)
        )
        value = jnp.zeros((rows, HD), jnp.float32)
        for lower in range(0, width, HD):
            scores = lax.dot_general(
                queries_ref[:, lower : lower + HD],
                keys,
                (((1,), (1,)), ((), ())),
                preferred_element_type=jnp.float32,
            )
            last = jnp.where(allowed, scores[:, whole:], -1e30)
            scores = jnp.concatenate([scores[:, :whole], last], axis=1) if whole else last
            top = jnp.max(scores, axis=1, keepdims=True)
            weights = jnp.exp2((scores - top) * factor).astype(jnp.bfloat16)
            mixed = jnp.dot(weights, values, preferred_element_type=jnp.float32)
            out = (mixed[:, :HD] / mixed[:, HD:]).astype(jnp.bfloat16)
            out_ref[:rows, lower : lower + HD] = out
            value = value + out.astype(jnp.float32) * head_ref[:, lower : lower + HD]
        total = lax.dot_general(
            jnp.ones((16, HD), jnp.float32),
            value,
            (((1,), (1,)), ((), ())),
            preferred_element_type=jnp.float32,
            precision=lax.Precision.HIGHEST,
        )
        if value_ref:
            value_ref[0][...] = total
        else:
            row = lax.broadcasted_iota(jnp.int32, total.shape, 0)
            high = total.astype(jnp.bfloat16).astype(jnp.float32)
            middle = (total - high).astype(jnp.bfloat16).astype(jnp.float32)
            pieces = jnp.where(row == 0, high, jnp.where(row == 1, middle, total - high - middle))
            out_ref[rows:, :HD] = pieces.astype(jnp.bfloat16)
            out_ref[rows:, HD:] = jnp.zeros((16, width - HD), jnp.bfloat16)

    for i in range(length // CHUNK):

        @pl.when(first // CHUNK == i)
        def _():
            attend_first((i + 1) * CHUNK)


def attend(first, queries, keys_values, head, sums_apart):
    rows, width = queries.shape
    length = keys_values.shape[0]
    vmem = pl.BlockSpec(memory_space=pltpu.VMEM)
    out_shape = [jax.ShapeDtypeStruct((rows if sums_apart else rows + 16, width), jnp.bfloat16)]
    if sums_apart:
        out_shape.append(jax.ShapeDtypeStruct((16, rows), jnp.float32))
    return pl.pallas_call(
        attend_kernel,
        out_shape=out_shape,
        in_specs=[pl.BlockSpec(memory_space=pltpu.SMEM), vmem, vmem, vmem],
        out_specs=[vmem] * len(out_shape),
        compiler_params=pltpu.CompilerParams(vmem_limit_bytes=32 * 2**20),
        cost_estimate=pl.CostEstimate(
            flops=4 * rows * width * length, bytes_accessed=4 * rows * width, transcendentals=rows * width * length // HD
        ),
    )(first, queries, keys_values, head)


def body(queries, keys_text, values_text, patch_rows, patch_owner, patch_place, value_head):
    rows = queries.shape[1]
    half = queries.shape[2] // 2
    dp_count = lax.axis_size("dp")
    chip_count = lax.axis_size("xh") * lax.axis_size("y")
    core = lax.axis_index("co")
    chip = lax.axis_index("xh") * lax.axis_size("y") + lax.axis_index("y")
    swap = [(0, 1), (1, 0)]
    count = patch_rows.shape[2]

    packed = pack(
        patch_rows[0, 0],
        patch_owner.reshape(1, count),
        patch_place.reshape(1, count),
        dp_count,
    )
    arrived = lax.all_to_all(packed.reshape(dp_count, CAP * 2, 3 * HD), "dp", 0, 0, tiled=True)
    arrived = arrived.reshape(dp_count * CAP * 2, 3 * HD)
    other_queries = lax.dynamic_slice_in_dim(queries[0], (1 - core) * half, half, 1)
    own_queries = lax.dynamic_slice_in_dim(queries[0], core * half, half, 1)
    got_queries = lax.ppermute(other_queries, "co", swap)
    head = lax.dynamic_slice_in_dim(value_head, core * half, half, 0)[None].astype(jnp.float32)
    text = jnp.concatenate([keys_text[0], values_text[0]], axis=1)
    arrived, got_queries, own_queries, head, text = lax.optimization_barrier(
        (arrived, got_queries, own_queries, head, text)
    )

    code = arrived[:, 2 * HD].astype(jnp.int32)
    is_value = jnp.arange(code.shape[0], dtype=jnp.int32) % 2
    lands = (jnp.arange(rows, dtype=jnp.int32)[:, None] + 1) == code[None, :]

    def added(wanted):
        landing = jnp.where(lands & (is_value == wanted)[None, :], 1.0, 0.0).astype(jnp.bfloat16)
        return jnp.dot(landing, arrived[:, : 2 * HD], preferred_element_type=jnp.float32)

    merged_keys = (text[:, : 2 * HD].astype(jnp.float32) + added(0)).astype(jnp.bfloat16)
    merged_values = (text[:, 2 * HD :].astype(jnp.float32) + added(1)).astype(jnp.bfloat16)

    def of_head(which):
        return jnp.concatenate(
            [
                jnp.where(which == 0, tensor[:, :HD], tensor[:, HD:])
                for tensor in (merged_keys, merged_values)
            ],
            axis=1,
        )

    own_merged = of_head(core)
    got_merged = lax.ppermute(of_head(1 - core), "co", swap)
    merged = jnp.where(
        core == 0,
        jnp.concatenate([own_merged, got_merged], axis=0),
        jnp.concatenate([got_merged, own_merged], axis=0),
    )
    wide = jnp.broadcast_to(merged[None], (chip_count, *merged.shape))
    start = chip * (2 * rows)
    firsts = (start + (1 - core) * rows)[None], (start + core * rows)[None]
    wide, got_queries, own_queries, head, firsts = lax.optimization_barrier(
        (wide, got_queries, own_queries, head, firsts)
    )
    keys_values = lax.all_to_all(wide, ("xh", "y"), 0, 0, tiled=True)
    keys_values = keys_values.reshape(chip_count * 2 * rows, 2 * HD)

    (other_out,) = attend(firsts[0], got_queries, keys_values, head, False)
    own_out, own_value = attend(firsts[1], own_queries, keys_values, head, True)
    got_out = lax.ppermute(other_out, "co", swap)
    got_value = jnp.sum(got_out[rows : rows + 3, :HD].astype(jnp.float32), axis=0)
    attention = jnp.where(
        core == 0,
        jnp.concatenate([own_out, got_out[:rows]], axis=1),
        jnp.concatenate([got_out[:rows], own_out], axis=1),
    )
    partial_value = own_value[0] + got_value
    far_value = lax.ppermute(partial_value, "tp", swap)
    attention, far_value = lax.optimization_barrier((attention, far_value))
    return attention[None], (partial_value + far_value)[None]


def solution(mesh):
    dp, ctx, tp = mesh.devices.shape
    wide = Mesh(mesh.devices.reshape(dp, 2, ctx // 4, 2, tp), ("dp", "xh", "y", "co", "tp"))
    ctx = ("xh", "y", "co")
    in_specs = (
        P("dp", ctx, "tp"),
        P("dp", ctx, "tp"),
        P("dp", ctx, "tp"),
        P("dp", ctx, None, None, "tp"),
        P("dp", ctx, None, None),
        P("dp", ctx, None),
        P("tp"),
    )
    out_specs = (P("dp", ctx, "tp"), P("dp", ctx))
    return jax.shard_map(body, mesh=wide, in_specs=in_specs, out_specs=out_specs, check_vma=False)
```

```python
import jax
import jax.numpy as jnp
from jax import lax
from jax.experimental import pallas as pl
from jax.experimental.pallas import tpu as pltpu
from jax.sharding import Mesh
from jax.sharding import PartitionSpec as P

HD = 128
CAP = 4
CHUNK = 256
LOG2E = 1.4426950408889634


def column(row):
    count = row.shape[1]
    same = lax.broadcasted_iota(jnp.int32, (count, count), 0) == lax.broadcasted_iota(
        jnp.int32, (count, count), 1
    )
    return jnp.sum(jnp.where(same, row, 0), axis=1, keepdims=True)


def pack_kernel(patch_ref, owner_ref, place_ref, out_ref):
    owner, place = owner_ref[...], place_ref[...]
    count = owner.shape[1]
    owner_column = column(owner)
    earlier = lax.broadcasted_iota(jnp.int32, (count, count), 0) < lax.broadcasted_iota(
        jnp.int32, (count, count), 1
    )
    rank = jnp.sum(jnp.where(earlier & (owner_column == owner), 1, 0), axis=0, keepdims=True)
    code = jnp.broadcast_to((column(place) + 1).astype(jnp.float32), (count, HD)).astype(jnp.bfloat16)
    slot = lax.broadcasted_iota(jnp.int32, (out_ref.shape[0] * CAP, count), 0)
    select = jnp.where(slot == owner * CAP + rank, 1.0, 0.0).astype(jnp.bfloat16)
    held = jnp.concatenate([patch_ref[:, 0, :], patch_ref[:, 1, :], code], axis=1)
    packed = jnp.dot(select, held, preferred_element_type=jnp.float32)
    out_ref[...] = packed.reshape(out_ref.shape).astype(jnp.bfloat16)


def pack(patch_rows, owner, place, sequences):
    vmem = pl.BlockSpec(memory_space=pltpu.VMEM)
    width = patch_rows.shape[1] * patch_rows.shape[2] + HD
    return pl.pallas_call(
        pack_kernel,
        out_shape=jax.ShapeDtypeStruct((sequences, CAP, width), jnp.bfloat16),
        in_specs=[vmem, vmem, vmem],
        out_specs=vmem,
    )(patch_rows, owner, place)


def merge_kernel(arrived_ref, keys_ref, values_ref, out_ref):
    arrived = arrived_ref[...].astype(jnp.float32)
    arrived = arrived.reshape(arrived.shape[0] * arrived.shape[1], arrived.shape[2])
    width = arrived.shape[1] - HD
    token = lax.broadcasted_iota(jnp.int32, (arrived.shape[0], HD), 1).astype(jnp.float32) + 1.0
    landing = jnp.where(arrived[:, width:] == token, 1.0, 0.0).astype(jnp.bfloat16)
    added = lax.dot_general(
        landing,
        arrived[:, :width].astype(jnp.bfloat16),
        (((0,), (0,)), ((), ())),
        preferred_element_type=jnp.float32,
    )
    text = jnp.concatenate([keys_ref[...], values_ref[...]], axis=1).astype(jnp.float32)
    merged = (text + added).astype(jnp.bfloat16)
    for chip in range(out_ref.shape[0]):
        out_ref[chip] = merged


def merge(arrived, keys_text, values_text, chips):
    vmem = pl.BlockSpec(memory_space=pltpu.VMEM)
    rows, width = keys_text.shape
    return pl.pallas_call(
        merge_kernel,
        out_shape=jax.ShapeDtypeStruct((chips, rows, 2 * width), jnp.bfloat16),
        in_specs=[vmem, vmem, vmem],
        out_specs=vmem,
        compiler_params=pltpu.CompilerParams(vmem_limit_bytes=8 * 2**20),
    )(arrived, keys_text, values_text)


def attend_kernel(place_ref, queries_ref, own_ref, got_ref, head_ref, out_ref, value_ref):
    rows, width = queries_ref.shape
    length = own_ref.shape[0]
    groups = own_ref.shape[1] // (2 * HD)
    heads = width // HD
    factor = HD ** (-0.5) * LOG2E
    chip, core = place_ref[0], place_ref[1]

    def attend_first(count):
        whole = count - CHUNK
        key = lax.broadcasted_iota(jnp.int32, (rows, CHUNK), 1) + whole
        query = lax.broadcasted_iota(jnp.int32, (rows, CHUNK), 0)
        block, spot = key // rows, key % rows
        own_allowed = (block < chip) | ((block == chip) & (spot <= query))
        got_allowed = block < chip + core
        value = jnp.zeros((rows, HD), jnp.float32)
        for h in range(heads):
            g = h // (heads // groups)
            queries = queries_ref[:, h * HD : (h + 1) * HD]
            scores = []
            for ref, allowed in ((own_ref, own_allowed), (got_ref, got_allowed)):
                part = lax.dot_general(
                    queries,
                    ref[:count, g * HD : (g + 1) * HD],
                    (((1,), (1,)), ((), ())),
                    preferred_element_type=jnp.float32,
                )
                if whole:
                    scores.append(part[:, :whole])
                scores.append(jnp.where(allowed, part[:, whole:], -1e30))
            scores = jnp.concatenate(scores, axis=1)
            top = jnp.max(scores, axis=1, keepdims=True)
            weights = jnp.exp2((scores - top) * factor).astype(jnp.bfloat16)
            lower = (groups + g) * HD
            values = jnp.concatenate(
                [own_ref[:count, lower : lower + HD], got_ref[:count, lower : lower + HD]], axis=0
            )
            values = jnp.concatenate([values, jnp.ones((2 * count, HD), jnp.bfloat16)], axis=1)
            mixed = jnp.dot(weights, values, preferred_element_type=jnp.float32)
            out = (mixed[:, :HD] / mixed[:, HD:]).astype(jnp.bfloat16)
            out_ref[:, h * HD : (h + 1) * HD] = out
            value = value + out.astype(jnp.float32) * head_ref[:, h * HD : (h + 1) * HD]
        value_ref[...] = lax.dot_general(
            jnp.ones((8, HD), jnp.float32),
            value,
            (((1,), (1,)), ((), ())),
            preferred_element_type=jnp.float32,
            precision=lax.Precision.HIGHEST,
        )

    for i in range(length // CHUNK):

        @pl.when(chip // (CHUNK // rows) == i)
        def _():
            attend_first((i + 1) * CHUNK)


def attend(place, queries, own, got, head):
    rows, width = queries.shape
    vmem = pl.BlockSpec(memory_space=pltpu.VMEM)
    pairs = 2 * rows * width * own.shape[0]
    return pl.pallas_call(
        attend_kernel,
        out_shape=(
            jax.ShapeDtypeStruct((rows, width), jnp.bfloat16),
            jax.ShapeDtypeStruct((8, rows), jnp.float32),
        ),
        in_specs=[pl.BlockSpec(memory_space=pltpu.SMEM), vmem, vmem, vmem, vmem],
        out_specs=(vmem, vmem),
        compiler_params=pltpu.CompilerParams(vmem_limit_bytes=40 * 2**20),
        cost_estimate=pl.CostEstimate(
            flops=4 * pairs, bytes_accessed=4 * rows * width, transcendentals=pairs // HD
        ),
    )(place, queries, own, got, head)


def body(queries, keys_text, values_text, patch_rows, patch_owner, patch_place, value_head):
    rows = queries.shape[1]
    dp_count = lax.axis_size("dp")
    chip_count = lax.axis_size("xh") * lax.axis_size("y")
    core = lax.axis_index("co")
    chip = lax.axis_index("xh") * lax.axis_size("y") + lax.axis_index("y")
    swap = [(0, 1), (1, 0)]
    count = patch_rows.shape[2]
    width = 2 * keys_text.shape[2]

    packed = pack(
        patch_rows[0, 0],
        patch_owner.reshape(1, count),
        patch_place.reshape(1, count),
        dp_count,
    )
    arrived = lax.all_to_all(packed, "dp", 0, 0, tiled=True)
    own_queries = queries[0]
    head = value_head[None].astype(jnp.float32)
    place = jnp.stack([chip, core])
    arrived, own_queries, head, place, keys_text, values_text = lax.optimization_barrier(
        (arrived, own_queries, head, place, keys_text, values_text)
    )
    wide = merge(arrived, keys_text[0], values_text[0], chip_count)
    wide, own_queries, head, place = lax.optimization_barrier((wide, own_queries, head, place))
    own = lax.all_to_all(wide, ("xh", "y"), 0, 0, tiled=True).reshape(chip_count * rows, width)
    got = lax.ppermute(own, "co", swap)
    attention, value = attend(place, own_queries, own, got, head)
    partial_value = value[0]
    value_out = partial_value + lax.ppermute(partial_value, "tp", swap)
    return attention[None], value_out[None]


def solution(mesh):
    dp, ctx, tp = mesh.devices.shape
    wide = Mesh(mesh.devices.reshape(dp, 2, ctx // 4, 2, tp), ("dp", "xh", "y", "co", "tp"))
    ctx = ("xh", "y", "co")
    in_specs = (
        P("dp", ctx, "tp"),
        P("dp", ctx, "tp"),
        P("dp", ctx, "tp"),
        P("dp", ctx, None, None, "tp"),
        P("dp", ctx, None, None),
        P("dp", ctx, None),
        P("tp"),
    )
    out_specs = (P("dp", ctx, "tp"), P("dp", ctx))
    return jax.shard_map(body, mesh=wide, in_specs=in_specs, out_specs=out_specs, check_vma=False)
```

```python
import jax
import jax.numpy as jnp
from jax import lax
from jax.experimental import pallas as pl
from jax.experimental.pallas import tpu as pltpu
from jax.sharding import Mesh
from jax.sharding import PartitionSpec as P

HD = 128
CAP = 4
CHUNK = 256
STACK = 2
LOG2E = 1.4426950408889634


def column(row):
    count = row.shape[1]
    same = lax.broadcasted_iota(jnp.int32, (count, count), 0) == lax.broadcasted_iota(
        jnp.int32, (count, count), 1
    )
    return jnp.sum(jnp.where(same, row, 0), axis=1, keepdims=True)


def pack_kernel(patch_ref, owner_ref, place_ref, out_ref):
    owner, place = owner_ref[...], place_ref[...]
    count = owner.shape[1]
    owner_column = column(owner)
    earlier = lax.broadcasted_iota(jnp.int32, (count, count), 0) < lax.broadcasted_iota(
        jnp.int32, (count, count), 1
    )
    rank = jnp.sum(jnp.where(earlier & (owner_column == owner), 1, 0), axis=0, keepdims=True)
    code = jnp.broadcast_to((column(place) + 1).astype(jnp.float32), (count, HD)).astype(jnp.bfloat16)
    slot = lax.broadcasted_iota(jnp.int32, (out_ref.shape[0] * CAP, count), 0)
    select = jnp.where(slot == owner * CAP + rank, 1.0, 0.0).astype(jnp.bfloat16)
    held = jnp.concatenate([patch_ref[:, 0, :], patch_ref[:, 1, :], code], axis=1)
    packed = jnp.dot(select, held, preferred_element_type=jnp.float32)
    out_ref[...] = packed.reshape(out_ref.shape).astype(jnp.bfloat16)


def pack(patch_rows, owner, place, sequences):
    vmem = pl.BlockSpec(memory_space=pltpu.VMEM)
    width = patch_rows.shape[1] * patch_rows.shape[2] + HD
    return pl.pallas_call(
        pack_kernel,
        out_shape=jax.ShapeDtypeStruct((sequences, CAP, width), jnp.bfloat16),
        in_specs=[vmem, vmem, vmem],
        out_specs=vmem,
    )(patch_rows, owner, place)


def merge_kernel(arrived_ref, keys_ref, values_ref, out_ref):
    arrived = arrived_ref[...].astype(jnp.float32)
    arrived = arrived.reshape(arrived.shape[0] * arrived.shape[1], arrived.shape[2])
    width = arrived.shape[1] - HD
    token = lax.broadcasted_iota(jnp.int32, (arrived.shape[0], HD), 1).astype(jnp.float32) + 1.0
    landing = jnp.where(arrived[:, width:] == token, 1.0, 0.0).astype(jnp.bfloat16)
    added = lax.dot_general(
        landing,
        arrived[:, :width].astype(jnp.bfloat16),
        (((0,), (0,)), ((), ())),
        preferred_element_type=jnp.float32,
    )
    text = jnp.concatenate([keys_ref[...], values_ref[...]], axis=1).astype(jnp.float32)
    merged = (text + added).astype(jnp.bfloat16)
    for chip in range(out_ref.shape[0]):
        out_ref[chip] = merged


def merge(arrived, keys_text, values_text, chips):
    vmem = pl.BlockSpec(memory_space=pltpu.VMEM)
    rows, width = keys_text.shape
    return pl.pallas_call(
        merge_kernel,
        out_shape=jax.ShapeDtypeStruct((chips, rows, 2 * width), jnp.bfloat16),
        in_specs=[vmem, vmem, vmem],
        out_specs=vmem,
        compiler_params=pltpu.CompilerParams(vmem_limit_bytes=8 * 2**20),
    )(arrived, keys_text, values_text)


def attend_kernel(queries_ref, own_ref, got_ref, head_ref, out_ref, value_ref):
    rows, width = queries_ref.shape
    length = own_ref.shape[0]
    groups = own_ref.shape[1] // (2 * HD)
    heads = width // HD
    factor = HD ** (-0.5) * LOG2E
    chip = lax.axis_index("xh") * lax.axis_size("y") + lax.axis_index("y")
    core = lax.axis_index("co")

    def attend_first(count):
        whole = count - CHUNK
        key = lax.broadcasted_iota(jnp.int32, (STACK * rows, CHUNK), 1) + whole
        query = lax.broadcasted_iota(jnp.int32, (STACK * rows, CHUNK), 0) % rows
        block, spot = key // rows, key % rows
        own_allowed = (block < chip) | ((block == chip) & (spot <= query))
        got_allowed = block < chip + core
        value = jnp.zeros((rows, HD), jnp.float32)
        for g in range(groups):
            lower = (groups + g) * HD
            values = jnp.concatenate(
                [own_ref[:count, lower : lower + HD], got_ref[:count, lower : lower + HD]], axis=0
            )
            values = jnp.concatenate([values, jnp.ones((2 * count, HD), jnp.bfloat16)], axis=1)
            for first in range(g * heads // groups, (g + 1) * heads // groups, STACK):
                stack = range(first, first + STACK)
                queries = jnp.concatenate(
                    [queries_ref[:, h * HD : (h + 1) * HD] for h in stack], axis=0
                )
                scores = []
                for ref, allowed in ((own_ref, own_allowed), (got_ref, got_allowed)):
                    part = lax.dot_general(
                        queries,
                        ref[:count, g * HD : (g + 1) * HD],
                        (((1,), (1,)), ((), ())),
                        preferred_element_type=jnp.float32,
                    )
                    if whole:
                        scores.append(part[:, :whole])
                    scores.append(jnp.where(allowed, part[:, whole:], -1e30))
                scores = jnp.concatenate(scores, axis=1)
                top = jnp.max(scores, axis=1, keepdims=True)
                weights = jnp.exp2((scores - top) * factor).astype(jnp.bfloat16)
                mixed = jnp.dot(weights, values, preferred_element_type=jnp.float32)
                out = (mixed[:, :HD] / mixed[:, HD:]).astype(jnp.bfloat16)
                for i, h in enumerate(stack):
                    part = out[i * rows : (i + 1) * rows]
                    out_ref[:, h * HD : (h + 1) * HD] = part
                    value = value + part.astype(jnp.float32) * head_ref[
                        :, h * HD : (h + 1) * HD
                    ].astype(jnp.float32)
        value_ref[...] = lax.dot_general(
            jnp.ones((8, HD), jnp.float32),
            value,
            (((1,), (1,)), ((), ())),
            preferred_element_type=jnp.float32,
            precision=lax.Precision.HIGHEST,
        )

    for i in range(length // CHUNK):

        @pl.when(chip // (CHUNK // rows) == i)
        def _():
            attend_first((i + 1) * CHUNK)


def attend(queries, own, got, head):
    rows, width = queries.shape
    vmem = pl.BlockSpec(memory_space=pltpu.VMEM)
    pairs = 2 * rows * width * own.shape[0]
    return pl.pallas_call(
        attend_kernel,
        out_shape=(
            jax.ShapeDtypeStruct((rows, width), jnp.bfloat16),
            jax.ShapeDtypeStruct((8, rows), jnp.float32),
        ),
        in_specs=[vmem, vmem, vmem, vmem],
        out_specs=(vmem, vmem),
        compiler_params=pltpu.CompilerParams(vmem_limit_bytes=40 * 2**20),
        cost_estimate=pl.CostEstimate(
            flops=4 * pairs, bytes_accessed=4 * rows * width, transcendentals=pairs // HD
        ),
    )(queries, own, got, head)


def body(queries, keys_text, values_text, patch_rows, patch_owner, patch_place, value_head):
    rows = queries.shape[1]
    dp_count = lax.axis_size("dp")
    chip_count = lax.axis_size("xh") * lax.axis_size("y")
    swap = [(0, 1), (1, 0)]
    count = patch_rows.shape[2]
    width = 2 * keys_text.shape[2]

    packed = pack(
        patch_rows[0, 0],
        patch_owner.reshape(1, count),
        patch_place.reshape(1, count),
        dp_count,
    )
    arrived = lax.all_to_all(packed, "dp", 0, 0, tiled=True)
    wide = merge(arrived, keys_text[0], values_text[0], chip_count)
    own = lax.all_to_all(wide, ("xh", "y"), 0, 0, tiled=True).reshape(chip_count * rows, width)
    got = lax.ppermute(own, "co", swap)
    attention, value = attend(queries[0], own, got, value_head[None])
    return attention[None], lax.psum(value[:1], "tp")


def solution(mesh):
    dp, ctx, tp = mesh.devices.shape
    wide = Mesh(mesh.devices.reshape(dp, 2, ctx // 4, 2, tp), ("dp", "xh", "y", "co", "tp"))
    ctx = ("xh", "y", "co")
    in_specs = (
        P("dp", ctx, "tp"),
        P("dp", ctx, "tp"),
        P("dp", ctx, "tp"),
        P("dp", ctx, None, None, "tp"),
        P("dp", ctx, None, None),
        P("dp", ctx, None),
        P("tp"),
    )
    out_specs = (P("dp", ctx, "tp"), P("dp", ctx))
    return jax.shard_map(body, mesh=wide, in_specs=in_specs, out_specs=out_specs, check_vma=False)
```
